32 devices in a mesh: stn: 8 (over z, y), grid: 4 (over x, core).
Axes of the slice: x: 2, y: 2, z: 4, core: 2. Of those that a mesh axis runs over, the one named last changes fastest.
Arguments:
- voltages: bfloat16 [512, 2, 12288], P('stn', None, 'grid'), may hold values from -6 to 6
- pfb_coeffs: float32 [16, 48], replicated, may hold values from -1.5 to 1.5
- station_offsets: int32 [2, 512], replicated, may hold values from 0 to 4
- tile_cells: int32 [24, 2, 136], P('stn'), may hold values from 0 to 127, as said below
- kernel_table: float32 [8, 7], replicated, may hold values from 0.2 to 1
Outputs:
- uv_grid: float32 [128, 24, 256], P('grid', 'stn')
The draws below stay inside these ranges and needn't reach their ends.
Inputs may be any that keep to these rules, and one draw needn't show every extreme that they name: tile_cells[c, 0, k] lies in one of the strips of 32 rows; in every channel at most 68 baseline tiles have their base row in the same strip, and one strip holds exactly 68. A base row in the last strip and every base column are at most 112.
All inputs are finite; a program needn't handle non-finite values.
Results may differ from the reference program's by a relative error of at most 0.0065.
Values may be sent and summed in bfloat16 or wider, within the bound.
A program may use at most 128 MiB of HBM per device.

```python
import math
import jax
import jax.numpy as jnp
import numpy as np
from jax import lax

STATIONS = 512
POLS = 2
CHANNELS = 24
FRAME = 48
TAPS = 16
SPECTRA = 256
TILE = 32
NPAIR = 136
PATCH = 16
KERN = 7
OVER = 8
SPREAD = 5
UV = 128
N_GRID = 4


def draw_tile_cells(key, part):
    subkeys = jax.random.split(key, 5)
    strip_rows = UV // N_GRID
    hot_count = NPAIR // 2
    hot_strip = jax.random.randint(subkeys[0], (CHANNELS, 1), 0, N_GRID)
    scores = jax.random.randint(subkeys[1], (CHANNELS, NPAIR), 0, 1 << 20) * NPAIR + jnp.arange(NPAIR, dtype=jnp.int32)[None, :]
    pair_rank = jnp.argsort(jnp.argsort(scores, axis=1), axis=1)
    other_step = jax.random.randint(subkeys[2], (CHANNELS, NPAIR), 1, N_GRID)
    owner_strip = jnp.where(pair_rank < hot_count, hot_strip, (hot_strip + other_step) % N_GRID)
    within = jax.random.randint(subkeys[3], (CHANNELS, NPAIR), 0, strip_rows)
    within = jnp.where(owner_strip == N_GRID - 1, within % (strip_rows - PATCH + 1), within)
    base_rows = owner_strip * strip_rows + within
    base_cols = jax.random.randint(subkeys[4], (CHANNELS, NPAIR), 0, UV - PATCH + 1)
    return jnp.stack([base_rows, base_cols], axis=1).astype(jnp.int32)


def with_ends(drawn, key, least, high):
    shape = drawn.shape
    spot = [jax.random.randint(jax.random.fold_in(key, axis), (), 0, shape[axis]) for axis in range(len(shape))]
    drawn = drawn.at[tuple(spot)].set(least)
    longest = shape.index(max(shape))
    spot[longest] = (spot[longest] + 1) % shape[longest]
    return drawn.at[tuple(spot)].set(high)


def levels(rng, shape, shards, smallest, high):
    factor_of, own = 1.0, jax.random.fold_in(rng, 6)
    for dim, blocks in shards:
        steps = jnp.exp(jax.random.uniform(jax.random.fold_in(own, dim), (blocks,), jnp.float32, smallest / len(shards), high / len(shards)))
        factor_of = factor_of * jnp.repeat(steps, shape[dim] // blocks).reshape([-1 if axis == dim else 1 for axis in range(len(shape))])
    return factor_of


def normal_values(stream_key, extent, spread, limit, pieces=(), kind=jnp.bfloat16):
    level = levels(stream_key, extent, pieces, -0.22, 0.18) if pieces else 1.0
    drawn = jax.random.normal(stream_key, extent, jnp.float32) * spread * level
    return jnp.minimum(jnp.maximum(drawn, -limit), limit).astype(kind)


def setup_inputs(seed: int = 0) -> dict:
    keys = jax.random.split(jax.random.key(seed), 6)
    return {
        "voltages": normal_values(keys[0], (STATIONS, POLS, SPECTRA * FRAME), 1.0, 6.0, ((0, 8), (2, 4))),
        "pfb_coeffs": normal_values(keys[1], (TAPS, FRAME), TAPS ** -0.5, 1.5, (), jnp.float32),
        "station_offsets": with_ends(jax.random.randint(keys[2], (2, STATIONS), 0, SPREAD), jax.random.fold_in(keys[2], 1), 0, SPREAD - 1).astype(jnp.int32),
        "tile_cells": draw_tile_cells(jax.random.fold_in(keys[5], 71), 0),
        "kernel_table": jnp.clip(jax.random.uniform(keys[4], (OVER, KERN), jnp.float32, 0.2, 1.0), 0.2, 1.0),
    }


highest = lax.Precision.HIGHEST

def dft_table(frame_len):
    chan_count = frame_len // 2
    sample_line = jnp.arange(frame_len, dtype=jnp.int32)[:, None]
    chan_line = jnp.arange(chan_count, dtype=jnp.int32)[None, :]
    angles = (sample_line * chan_line % frame_len).astype(jnp.float32) * (2.0 * math.pi / frame_len)
    norm_factor = 1.0 / math.sqrt(frame_len)
    twiddle = jnp.stack([jnp.cos(angles) * norm_factor, -jnp.sin(angles) * norm_factor], axis=2)
    return twiddle.reshape(frame_len, 2 * chan_count).astype(jnp.bfloat16)

def filter_frames(frames, coeffs, spec_count):
    summed = jnp.zeros(frames.shape[:2] + (spec_count, frames.shape[3]), jnp.float32)
    for tap_index in range(coeffs.shape[0]):
        summed = summed + coeffs[tap_index] * frames[:, :, tap_index:tap_index + spec_count, :].astype(jnp.float32)
    return summed.astype(jnp.bfloat16)

def pair_tables(tile_count):
    pair_first, pair_second = np.triu_indices(tile_count)
    return (jnp.asarray(pair_first.astype(np.int32)), jnp.asarray(pair_second.astype(np.int32)))

def correlate(spectrum, norm_factor):
    real_part, imag_part = (spectrum[0], spectrum[1])
    stacked = jnp.concatenate([jnp.concatenate([real_part, imag_part], axis=1), jnp.concatenate([imag_part, -real_part], axis=1)], axis=0)
    partner = jnp.concatenate([real_part, imag_part], axis=1)
    product = lax.dot_general(stacked, partner, (((1,), (1,)), ((), ())), preferred_element_type=jnp.float32)
    stations = real_part.shape[0]
    return product.reshape(2, stations, stations) * norm_factor

def axis_weights(offsets, first_stn, second_stn, frequency, divisor, kernel_table):
    over_count = kernel_table.shape[0]
    separation = offsets[first_stn][:, :, None] - offsets[second_stn][:, None, :] + (SPREAD - 1)
    scaled = separation * frequency
    cell_index = scaled // divisor
    fine_index = scaled % divisor * over_count // divisor
    choose = (fine_index[..., None] == jnp.arange(over_count, dtype=jnp.int32)).astype(jnp.float32)
    tap_values = jnp.einsum('kpqo,ot->kpqt', choose, kernel_table, precision=highest)
    place_rel = jnp.arange(PATCH, dtype=jnp.int32) - cell_index[..., None]
    weights = jnp.zeros(place_rel.shape, jnp.float32)
    for tap_index in range(kernel_table.shape[1]):
        weights = weights + tap_values[..., tap_index:tap_index + 1] * (place_rel == tap_index).astype(jnp.float32)
    return weights.reshape(weights.shape[0], -1, PATCH)

def make_patches(vis_real, vis_imag, first_stn, second_stn, offsets, frequency, divisor, kernel_table):
    weight_u = axis_weights(offsets[0], first_stn, second_stn, frequency, divisor, kernel_table)
    weight_v = axis_weights(offsets[1], first_stn, second_stn, frequency, divisor, kernel_table)
    keep_mask = (first_stn[:, :, None] < second_stn[:, None, :]).astype(jnp.float32).reshape(first_stn.shape[0], -1)
    real_kept = vis_real.reshape(keep_mask.shape) * keep_mask
    imag_kept = vis_imag.reshape(keep_mask.shape) * keep_mask
    weighted = jnp.concatenate([weight_v * real_kept[..., None], weight_v * imag_kept[..., None]], axis=2)
    return jnp.einsum('kbr,kbs->krs', weight_u, weighted, precision=highest)

def place_patches(uv_plane, patches, base_rows, base_cols):
    patch_line = jnp.arange(PATCH, dtype=jnp.int32)
    row_index = base_rows[:, None] + patch_line[None, :]
    col_index = jnp.concatenate([base_cols[:, None] + patch_line[None, :], UV + base_cols[:, None] + patch_line[None, :]], axis=1)
    return uv_plane.at[row_index[:, :, None], col_index[:, None, :]].add(patches, mode='drop')

def grid_pairs(visibility, base_cells, frequency, offsets, kernel_table, divisor):
    stations = visibility.shape[1]
    tile_count = stations // TILE
    vis_tiles = visibility.reshape(2, tile_count, TILE, tile_count, TILE)
    pair_first, pair_second = pair_tables(tile_count)
    pair_block = tile_count + 1
    tile_line = jnp.arange(TILE, dtype=jnp.int32)

    def add_block(uv_plane, block_index):
        block_start = (block_index * pair_block).astype(jnp.int32)
        first_tile = lax.dynamic_slice_in_dim(pair_first, block_start, pair_block)
        second_tile = lax.dynamic_slice_in_dim(pair_second, block_start, pair_block)
        vis_real = vis_tiles[0][first_tile, :, second_tile, :]
        vis_imag = vis_tiles[1][first_tile, :, second_tile, :]
        first_stn = first_tile[:, None] * TILE + tile_line[None, :]
        second_stn = second_tile[:, None] * TILE + tile_line[None, :]
        patches = make_patches(vis_real, vis_imag, first_stn, second_stn, offsets, frequency, divisor, kernel_table)
        base_rows = lax.dynamic_slice_in_dim(base_cells[0], block_start, pair_block)
        base_cols = lax.dynamic_slice_in_dim(base_cells[1], block_start, pair_block)
        return (place_patches(uv_plane, patches, base_rows, base_cols), None)
    uv_plane, _ = lax.scan(add_block, jnp.zeros((UV, 2 * UV), jnp.float32), jnp.arange(pair_first.shape[0] // pair_block, dtype=jnp.int32))
    return uv_plane

def station_spectra(station_volts, pfb_coeffs, twiddle):
    frame_len = pfb_coeffs.shape[1]
    tap_count = pfb_coeffs.shape[0]
    spec_count = station_volts.shape[1] // frame_len
    frames = station_volts.reshape(1, station_volts.shape[0], spec_count, frame_len)
    padded = jnp.concatenate([jnp.zeros((1, station_volts.shape[0], tap_count - 1, frame_len), station_volts.dtype), frames], axis=2)
    filtered = filter_frames(padded, pfb_coeffs, spec_count).reshape(-1, frame_len)
    return lax.dot_general(twiddle, filtered, (((0,), (1,)), ((), ())), preferred_element_type=jnp.float32).astype(jnp.bfloat16)

def reference(voltages, pfb_coeffs, station_offsets, tile_cells, kernel_table):
    twiddle = dft_table(FRAME)
    spectra = lax.map(lambda station_volts: station_spectra(station_volts, pfb_coeffs, twiddle), voltages)
    spectra = jnp.transpose(spectra, (1, 0, 2)).reshape(CHANNELS, 2, STATIONS, -1)
    norm_factor = 1.0 / (POLS * SPECTRA)
    divisor = FRAME - 1

    def channel_plane(chan_index):
        visibility = correlate(spectra[chan_index], norm_factor)
        return grid_pairs(visibility, tile_cells[chan_index], CHANNELS + chan_index, station_offsets, kernel_table, divisor)
    planes = lax.map(channel_plane, jnp.arange(CHANNELS, dtype=jnp.int32))
    return jnp.transpose(planes, (1, 0, 2))
```

```python
import math

import jax
import jax.numpy as jnp
import numpy as np
from jax import lax
from jax.sharding import PartitionSpec as P

TILE = 32
PATCH = 16
SPREAD = 5
UV = 128


highest = lax.Precision.HIGHEST


def shifted(block, axis, distance):
    devices = range(lax.axis_size(axis))
    route = [(i - distance, i) for i in devices if i - distance in devices]
    return lax.ppermute(block, axis, route)


def dft_table(frame_len):
    chan_count = frame_len // 2
    sample_line = jnp.arange(frame_len, dtype=jnp.int32)[:, None]
    chan_line = jnp.arange(chan_count, dtype=jnp.int32)[None, :]
    angles = (sample_line * chan_line % frame_len).astype(jnp.float32) * (2.0 * math.pi / frame_len)
    norm_factor = 1.0 / math.sqrt(frame_len)
    twiddle = jnp.stack([jnp.cos(angles) * norm_factor, -jnp.sin(angles) * norm_factor], axis=2)
    return twiddle.reshape(frame_len, 2 * chan_count).astype(jnp.bfloat16)


CLASSES = 32
high = lax.Precision.HIGH


def fused_filter(coeffs, twiddle, step):
    taps, frame_len = coeffs.shape
    flat = coeffs.reshape(-1)
    columns = [
        jnp.pad(flat, (frame_len * (f + 1), frame_len * (step - 1 - f))) for f in range(step)
    ]
    shifted_coeffs = jnp.stack(columns, axis=0)
    spread = np.kron(np.ones((1, frame_len), np.float32), np.eye(step, dtype=np.float32))
    wide = jnp.einsum("fm,fn->mn", shifted_coeffs, jnp.asarray(spread), precision=highest)
    tiled = jnp.tile(jnp.repeat(twiddle.astype(jnp.float32), step, axis=1), (step + taps, 1))
    return (wide * tiled).astype(jnp.bfloat16)

def separation_table(frequency, divisor, kernel_table):
    over_count = kernel_table.shape[0]
    separation = jnp.arange(2 * SPREAD - 1, dtype=jnp.int32)
    scaled = separation * frequency
    cell_index = scaled // divisor
    fine_index = scaled % divisor * over_count // divisor
    choose = (fine_index[:, None] == jnp.arange(over_count, dtype=jnp.int32)[None, :]).astype(
        jnp.float32
    )
    tap_values = jnp.dot(choose, kernel_table, precision=highest)
    place_rel = jnp.arange(PATCH, dtype=jnp.int32)[None, :] - cell_index[:, None]
    weights = jnp.zeros(place_rel.shape, jnp.float32)
    for tap_index in range(kernel_table.shape[1]):
        weights = weights + tap_values[:, tap_index : tap_index + 1] * (
            place_rel == tap_index
        ).astype(jnp.float32)
    return weights


def joint_weights(frequencies, divisor, kernel_table):
    class_line = np.arange(CLASSES)
    class_u = np.minimum(class_line // SPREAD, SPREAD - 1)
    class_v = class_line % SPREAD
    sep_line = np.arange(2 * SPREAD - 1)
    pick_u = (class_u[:, None] - class_u[None, :] + SPREAD - 1).reshape(-1, 1) == sep_line
    pick_v = (class_v[:, None] - class_v[None, :] + SPREAD - 1).reshape(-1, 1) == sep_line
    weights = jnp.stack([separation_table(f, divisor, kernel_table) for f in frequencies])
    over_r = np.kron(np.eye(PATCH), np.ones((1, PATCH))).astype(np.float32)
    over_t = np.kron(np.ones((1, PATCH)), np.eye(PATCH)).astype(np.float32)
    wide_u = jnp.einsum("czr,rm->czm", weights, jnp.asarray(over_r), precision=highest)
    wide_v = jnp.einsum("czr,rm->czm", weights, jnp.asarray(over_t), precision=highest)
    full_u = jnp.einsum("qz,czm->cqm", jnp.asarray(pick_u.astype(np.float32)), wide_u, precision=highest)
    full_v = jnp.einsum("qz,czm->cqm", jnp.asarray(pick_v.astype(np.float32)), wide_v, precision=highest)
    return full_u * full_v


def body(voltages, pfb_coeffs, station_offsets, tile_cells, kernel_table):
    stn_local, pol_count, samples = voltages.shape
    tap_count, frame_len = pfb_coeffs.shape
    spec_count = samples // frame_len
    step = 128 // math.gcd(128, frame_len)
    chunks = spec_count // step
    flat = voltages.reshape(stn_local * pol_count, samples)
    earlier = shifted(flat[:, samples - tap_count * frame_len :], "grid", 1)
    extended = jnp.concatenate([earlier, flat], axis=1)
    width = step * frame_len
    reach = (step + tap_count) * frame_len
    blocks = jnp.stack(
        [extended[:, c * width : c * width + reach] for c in range(chunks)], axis=1
    )
    matrix = fused_filter(pfb_coeffs, dft_table(frame_len), step)
    spectra = jnp.einsum(
        "rcm,mn->nrc", blocks, matrix, preferred_element_type=jnp.float32
    ).astype(jnp.bfloat16)
    spectra = spectra.reshape(frame_len // 2, 2, step, stn_local, pol_count * chunks)
    spectra = jnp.transpose(spectra, (0, 1, 3, 2, 4)).reshape(
        frame_len // 2, 2, stn_local, step * pol_count * chunks
    )
    turned = lax.all_to_all(spectra, "stn", split_axis=0, concat_axis=2, tiled=True)
    ch_dev, _, stations, depth = turned.shape
    tiles = stations // TILE
    divisor = frame_len - 1
    first_chan = lax.axis_index("stn") * ch_dev + frame_len // 2
    norm_factor = 1.0 / (pol_count * spec_count * lax.axis_size("grid"))

    classes = (station_offsets[0] * SPREAD + station_offsets[1]).reshape(tiles, TILE)
    hot = classes[:, :, None] == jnp.arange(CLASSES, dtype=jnp.int32)
    hot_low = hot.astype(jnp.bfloat16)
    hot_full = hot.astype(jnp.float32)
    tiled = turned.reshape(ch_dev, 2, tiles, TILE, depth)
    summed = jnp.einsum(
        "aiq,ceaik->ceaqk", hot_low, tiled, preferred_element_type=jnp.float32
    ).astype(jnp.bfloat16)

    def stacked(z):
        real_part, imag_part = z[:, 0], z[:, 1]
        partner = jnp.concatenate([real_part, imag_part], axis=-1)
        turned_partner = jnp.concatenate([imag_part, -real_part], axis=-1)
        return jnp.stack([partner, turned_partner], axis=1), partner

    left, right = stacked(summed)
    cross = jnp.einsum("ceaqk,cbsk->ceabqs", left, right, preferred_element_type=jnp.float32)
    joint = joint_weights([first_chan + i for i in range(ch_dev)], divisor, kernel_table)
    joint = joint * norm_factor
    patch = jnp.einsum(
        "ceabm,cmn->ceabn",
        cross.reshape(ch_dev, 2, tiles, tiles, CLASSES * CLASSES),
        joint,
        precision=high,
    )
    own_left, own_right = stacked(tiled)
    own = jnp.einsum("ceaik,cajk->ceaij", own_left, own_right, preferred_element_type=jnp.float32)
    line = np.arange(TILE)
    own = jnp.where(jnp.asarray(line[:, None] < line[None, :]), own, 0.0)
    own = jnp.einsum("aiq,ceaij->ceaqj", hot_full, own, precision=high)
    own = jnp.einsum("ceaqj,ajs->ceaqs", own, hot_full, precision=high)
    own_patch = jnp.einsum(
        "ceam,cmn->cean", own.reshape(ch_dev, 2, tiles, CLASSES * CLASSES), joint, precision=high
    )
    same = np.eye(tiles, dtype=bool)[:, :, None]
    patch = jnp.where(jnp.asarray(same), own_patch[:, :, :, None, :], patch)

    pair_first, pair_second = np.triu_indices(tiles)
    select = np.zeros((pair_first.size, tiles * tiles), np.float32)
    select[np.arange(pair_first.size), pair_first * tiles + pair_second] = 1.0
    missing = (1.0 - select.sum(axis=0)).astype(np.int32) * 4096
    cells = jnp.einsum(
        "cxk,kp->cxp", tile_cells.astype(jnp.float32), jnp.asarray(select), precision=highest
    )
    cells = jnp.round(cells).astype(jnp.int32) + jnp.asarray(missing)
    patch = patch.reshape(ch_dev, 2, tiles * tiles, PATCH, PATCH)
    patch_line = jnp.arange(PATCH, dtype=jnp.int32)
    target = cells[..., None] + patch_line
    spots = (target[..., None] == jnp.arange(UV, dtype=jnp.int32)).astype(jnp.float32)
    rows, cols = spots[:, 0], spots[:, 1]
    spread_cols = jnp.einsum("cekrt,cktw->ckrew", patch, cols, precision=high)
    planes = jnp.einsum("ckru,ckrew->ucew", rows, spread_cols, precision=high)
    planes = planes.reshape(UV, ch_dev, 2 * UV)
    return lax.psum_scatter(planes, "grid", scatter_dimension=0, tiled=True)


def solution(mesh):
    placed = (P("stn", None, "grid"), P(), P(), P("stn", None, None), P())
    return jax.shard_map(
        body, mesh=mesh, in_specs=placed, out_specs=P("grid", "stn", None), check_vma=False
    )
```

```python
import math

import jax
import jax.numpy as jnp
import numpy as np
from jax import lax
from jax.sharding import PartitionSpec as P

TILE = 32
PATCH = 16
SPREAD = 5
UV = 128


highest = lax.Precision.HIGHEST


def shifted(block, axis, distance):
    devices = range(lax.axis_size(axis))
    route = [(i - distance, i) for i in devices if i - distance in devices]
    return lax.ppermute(block, axis, route)


def dft_table(frame_len):
    chan_count = frame_len // 2
    sample_line = jnp.arange(frame_len, dtype=jnp.int32)[:, None]
    chan_line = jnp.arange(chan_count, dtype=jnp.int32)[None, :]
    angles = (sample_line * chan_line % frame_len).astype(jnp.float32) * (2.0 * math.pi / frame_len)
    norm_factor = 1.0 / math.sqrt(frame_len)
    twiddle = jnp.stack([jnp.cos(angles) * norm_factor, -jnp.sin(angles) * norm_factor], axis=2)
    return twiddle.reshape(frame_len, 2 * chan_count).astype(jnp.bfloat16)


CLASSES = 32
high = lax.Precision.HIGH


def fused_filter(coeffs, twiddle, step):
    taps, frame_len = coeffs.shape
    flat = coeffs.reshape(-1)
    columns = [
        jnp.pad(flat, (frame_len * (f + 1), frame_len * (step - 1 - f))) for f in range(step)
    ]
    shifted_coeffs = jnp.stack(columns, axis=0)
    spread = np.kron(np.ones((1, frame_len), np.float32), np.eye(step, dtype=np.float32))
    wide = jnp.einsum("fm,fn->mn", shifted_coeffs, jnp.asarray(spread), precision=highest)
    tiled = jnp.tile(jnp.repeat(twiddle.astype(jnp.float32), step, axis=1), (step + taps, 1))
    return (wide * tiled).astype(jnp.bfloat16)

def separation_table(frequency, divisor, kernel_table):
    over_count = kernel_table.shape[0]
    separation = jnp.arange(2 * SPREAD - 1, dtype=jnp.int32)
    scaled = separation * frequency
    cell_index = scaled // divisor
    fine_index = scaled % divisor * over_count // divisor
    choose = (fine_index[:, None] == jnp.arange(over_count, dtype=jnp.int32)[None, :]).astype(
        jnp.float32
    )
    tap_values = jnp.dot(choose, kernel_table, precision=highest)
    place_rel = jnp.arange(PATCH, dtype=jnp.int32)[None, :] - cell_index[:, None]
    weights = jnp.zeros(place_rel.shape, jnp.float32)
    for tap_index in range(kernel_table.shape[1]):
        weights = weights + tap_values[:, tap_index : tap_index + 1] * (
            place_rel == tap_index
        ).astype(jnp.float32)
    return weights


def joint_weights(frequencies, divisor, kernel_table):
    class_line = np.arange(CLASSES)
    class_u = np.minimum(class_line // SPREAD, SPREAD - 1)
    class_v = class_line % SPREAD
    sep_line = np.arange(2 * SPREAD - 1)
    pick_u = (class_u[None, :] - class_u[:, None] + SPREAD - 1).reshape(-1, 1) == sep_line
    pick_v = (class_v[None, :] - class_v[:, None] + SPREAD - 1).reshape(-1, 1) == sep_line
    weights = jnp.stack([separation_table(f, divisor, kernel_table) for f in frequencies])
    over_r = np.kron(np.eye(PATCH), np.ones((1, PATCH))).astype(np.float32)
    over_t = np.kron(np.ones((1, PATCH)), np.eye(PATCH)).astype(np.float32)
    wide_u = jnp.einsum("czr,rm->czm", weights, jnp.asarray(over_r), precision=highest)
    wide_v = jnp.einsum("czr,rm->czm", weights, jnp.asarray(over_t), precision=highest)
    full_u = jnp.einsum("qz,czm->cqm", jnp.asarray(pick_u.astype(np.float32)), wide_u, precision=highest)
    full_v = jnp.einsum("qz,czm->cqm", jnp.asarray(pick_v.astype(np.float32)), wide_v, precision=highest)
    return full_u * full_v


def body(voltages, pfb_coeffs, station_offsets, tile_cells, kernel_table):
    stn_local, pol_count, samples = voltages.shape
    tap_count, frame_len = pfb_coeffs.shape
    spec_count = samples // frame_len
    step = 128 // math.gcd(128, frame_len)
    chunks = spec_count // step
    flat = jnp.transpose(voltages, (1, 0, 2))
    earlier = shifted(flat[:, :, samples - tap_count * frame_len :], "grid", 1)
    extended = jnp.concatenate([earlier, flat], axis=2)
    width = step * frame_len
    reach = (step + tap_count) * frame_len
    blocks = jnp.stack(
        [extended[:, :, c * width : c * width + reach] for c in range(chunks)], axis=1
    )
    matrix = fused_filter(pfb_coeffs, dft_table(frame_len), step)
    spectra = jnp.einsum(
        "pcsm,mn->npcs", blocks, matrix, preferred_element_type=jnp.float32
    ).astype(jnp.bfloat16)
    spectra = spectra.reshape(frame_len // 2, 2, step * pol_count * chunks, stn_local)
    turned = lax.all_to_all(spectra, "stn", split_axis=0, concat_axis=3, tiled=True)
    turned = jnp.transpose(turned, (0, 1, 3, 2))
    ch_dev, _, stations, depth = turned.shape
    tiles = stations // TILE
    divisor = frame_len - 1
    first_chan = lax.axis_index("stn") * ch_dev + frame_len // 2
    norm_factor = 1.0 / (pol_count * spec_count * lax.axis_size("grid"))

    classes = (station_offsets[0] * SPREAD + station_offsets[1]).reshape(tiles, TILE)
    hot = classes[:, :, None] == jnp.arange(CLASSES, dtype=jnp.int32)
    hot_low = hot.astype(jnp.bfloat16)
    hot_full = hot.astype(jnp.float32)
    tiled = turned.reshape(ch_dev, 2, tiles, TILE, depth)
    summed = jnp.einsum(
        "aiq,ceaik->ceaqk", hot_low, tiled, preferred_element_type=jnp.float32
    ).astype(jnp.bfloat16)

    def stacked(z):
        real_part, imag_part = z[:, 0], z[:, 1]
        partner = jnp.concatenate([real_part, imag_part], axis=-1)
        turned_partner = jnp.concatenate([imag_part, -real_part], axis=-1)
        return jnp.stack([partner, turned_partner], axis=1), partner

    left, right = stacked(summed)
    cross = jnp.einsum("ceaqk,cbsk->ceabsq", left, right, preferred_element_type=jnp.float32)
    joint = joint_weights([first_chan + i for i in range(ch_dev)], divisor, kernel_table)
    joint = joint * norm_factor
    patch = jnp.einsum(
        "ceabm,cmn->ceabn",
        cross.reshape(ch_dev, 2, tiles, tiles, CLASSES * CLASSES),
        joint,
        precision=high,
    )
    own_left, own_right = stacked(tiled)
    own = jnp.einsum("ceaik,cajk->ceaij", own_left, own_right, preferred_element_type=jnp.float32)
    line = np.arange(TILE)
    own = jnp.where(jnp.asarray(line[:, None] < line[None, :]), own, 0.0)
    own = jnp.einsum("aiq,ceaij->ceaqj", hot_full, own, precision=high)
    own = jnp.einsum("ceaqj,ajs->ceasq", own, hot_full, precision=high)
    own_patch = jnp.einsum(
        "ceam,cmn->cean", own.reshape(ch_dev, 2, tiles, CLASSES * CLASSES), joint, precision=high
    )
    same = np.eye(tiles, dtype=bool)[:, :, None]
    patch = jnp.where(jnp.asarray(same), own_patch[:, :, :, None, :], patch)

    pair_first, pair_second = np.triu_indices(tiles)
    select = np.zeros((pair_first.size, tiles * tiles), np.float32)
    select[np.arange(pair_first.size), pair_first * tiles + pair_second] = 1.0
    missing = (1.0 - select.sum(axis=0)).astype(np.int32) * 4096
    cells = jnp.einsum(
        "cxk,kp->cxp", tile_cells.astype(jnp.float32), jnp.asarray(select), precision=highest
    )
    cells = jnp.round(cells).astype(jnp.int32) + jnp.asarray(missing)
    patch = patch.reshape(ch_dev, 2, tiles * tiles, PATCH, PATCH)
    patch_line = jnp.arange(PATCH, dtype=jnp.int32)
    target = cells[..., None] + patch_line
    spots = (target[..., None] == jnp.arange(UV, dtype=jnp.int32)).astype(jnp.float32)
    rows, cols = spots[:, 0], spots[:, 1]
    spread_cols = jnp.einsum("cekrt,cktw->ckrew", patch, cols, precision=high)
    planes = jnp.einsum("ckru,ckrew->ucew", rows, spread_cols, precision=high)
    planes = planes.reshape(UV, ch_dev, 2 * UV)
    return lax.psum_scatter(planes, "grid", scatter_dimension=0, tiled=True)


def solution(mesh):
    placed = (P("stn", None, "grid"), P(), P(), P("stn", None, None), P())
    return jax.shard_map(
        body, mesh=mesh, in_specs=placed, out_specs=P("grid", "stn", None), check_vma=False
    )
```

```python
import math

import jax
import jax.numpy as jnp
import numpy as np
from jax import lax
from jax.sharding import PartitionSpec as P

TILE = 32
PATCH = 16
SPREAD = 5
UV = 128


highest = lax.Precision.HIGHEST


def shifted(block, axis, distance):
    devices = range(lax.axis_size(axis))
    route = [(i - distance, i) for i in devices if i - distance in devices]
    return lax.ppermute(block, axis, route)


def dft_table(frame_len):
    chan_count = frame_len // 2
    sample_line = jnp.arange(frame_len, dtype=jnp.int32)[:, None]
    chan_line = jnp.arange(chan_count, dtype=jnp.int32)[None, :]
    angles = (sample_line * chan_line % frame_len).astype(jnp.float32) * (2.0 * math.pi / frame_len)
    norm_factor = 1.0 / math.sqrt(frame_len)
    twiddle = jnp.stack([jnp.cos(angles) * norm_factor, -jnp.sin(angles) * norm_factor], axis=2)
    return twiddle.reshape(frame_len, 2 * chan_count).astype(jnp.bfloat16)


CLASSES = SPREAD * SPREAD
high = lax.Precision.HIGH


def fused_filter(coeffs, twiddle, step):
    taps, frame_len = coeffs.shape
    flat = coeffs.reshape(-1)
    columns = [
        jnp.pad(flat, (frame_len * (f + 1), frame_len * (step - 1 - f))) for f in range(step)
    ]
    shifted_coeffs = jnp.stack(columns, axis=0)
    spread = np.kron(np.ones((1, frame_len), np.float32), np.eye(step, dtype=np.float32))
    wide = jnp.einsum("fm,fn->mn", shifted_coeffs, jnp.asarray(spread), precision=highest)
    tiled = jnp.tile(jnp.repeat(twiddle.astype(jnp.float32), step, axis=1), (step + taps, 1))
    return (wide * tiled).astype(jnp.bfloat16)

def separation_table(frequency, divisor, kernel_table):
    over_count = kernel_table.shape[0]
    separation = jnp.arange(2 * SPREAD - 1, dtype=jnp.int32)
    scaled = separation * frequency
    cell_index = scaled // divisor
    fine_index = scaled % divisor * over_count // divisor
    choose = (fine_index[:, None] == jnp.arange(over_count, dtype=jnp.int32)[None, :]).astype(
        jnp.float32
    )
    tap_values = jnp.dot(choose, kernel_table, precision=highest)
    place_rel = jnp.arange(PATCH, dtype=jnp.int32)[None, :] - cell_index[:, None]
    weights = jnp.zeros(place_rel.shape, jnp.float32)
    for tap_index in range(kernel_table.shape[1]):
        weights = weights + tap_values[:, tap_index : tap_index + 1] * (
            place_rel == tap_index
        ).astype(jnp.float32)
    return weights


def shifted_weights(weights, bases):
    place = jnp.arange(UV, dtype=jnp.int32)[None, :, None] - bases[:, None, :]
    taps = jnp.arange(PATCH, dtype=jnp.int32)[None, :, None, None]
    spots = (place[:, None] == taps).astype(jnp.float32)
    return jnp.einsum("cdt,ctwp->cdwp", weights, spots, precision=highest)


def body(voltages, pfb_coeffs, station_offsets, tile_cells, kernel_table):
    stn_local, pol_count, samples = voltages.shape
    tap_count, frame_len = pfb_coeffs.shape
    spec_count = samples // frame_len
    step = 128 // math.gcd(128, frame_len)
    chunks = spec_count // step
    flat = jnp.transpose(voltages, (1, 0, 2))
    earlier = shifted(flat[:, :, samples - tap_count * frame_len :], "grid", 1)
    extended = jnp.concatenate([earlier, flat], axis=2)
    width = step * frame_len
    reach = (step + tap_count) * frame_len
    blocks = jnp.stack(
        [extended[:, :, c * width : c * width + reach] for c in range(chunks)], axis=1
    )
    matrix = fused_filter(pfb_coeffs, dft_table(frame_len), step)
    spectra = jnp.einsum(
        "pcsm,mn->npcs", blocks, matrix, preferred_element_type=jnp.float32
    ).astype(jnp.bfloat16)
    spectra = spectra.reshape(frame_len // 2, 2, step * pol_count * chunks, stn_local)
    turned = lax.all_to_all(spectra, "stn", split_axis=0, concat_axis=3, tiled=True)
    turned = jnp.transpose(turned, (0, 1, 3, 2))
    ch_dev, _, stations, depth = turned.shape
    tiles = stations // TILE
    divisor = frame_len - 1
    first_chan = lax.axis_index("stn") * ch_dev + frame_len // 2
    norm_factor = 1.0 / (pol_count * spec_count * lax.axis_size("grid"))

    classes = (station_offsets[0] * SPREAD + station_offsets[1]).reshape(tiles, TILE)
    hot = classes[:, :, None] == jnp.arange(CLASSES, dtype=jnp.int32)
    hot_low = hot.astype(jnp.bfloat16)
    hot_full = hot.astype(jnp.float32)
    tiled = turned.reshape(ch_dev, 2, tiles, TILE, depth)
    summed = jnp.einsum(
        "aiq,ceaik->ceaqk", hot_low, tiled, preferred_element_type=jnp.float32
    ).astype(jnp.bfloat16)

    def stacked(z):
        real_part, imag_part = z[:, 0], z[:, 1]
        partner = jnp.concatenate([real_part, imag_part], axis=-1)
        turned_partner = jnp.concatenate([imag_part, -real_part], axis=-1)
        return jnp.stack([partner, turned_partner], axis=1), partner

    left, right = stacked(summed)
    shape = (SPREAD, SPREAD, 2 * depth)
    terms = []
    for i in range(ch_dev):
        taps = jnp.transpose(left[i].reshape((2 * tiles,) + shape), (1, 2, 3, 0))
        terms.append(
            lax.conv_general_dilated(
                right[i].reshape((tiles,) + shape),
                taps,
                (1, 1),
                [(SPREAD - 1, SPREAD - 1)] * 2,
                dimension_numbers=("NHWC", "HWIO", "HWNC"),
                preferred_element_type=jnp.float32,
            )
        )
    seps = 2 * SPREAD - 1
    cross = jnp.stack(terms).reshape(ch_dev, seps, seps, tiles, 2, tiles)
    cross = jnp.transpose(cross, (0, 4, 1, 2, 3, 5)).reshape(ch_dev, 2, seps, seps, tiles * tiles)
    own_left, own_right = stacked(tiled)
    own = jnp.einsum("ceaik,cajk->ceaij", own_left, own_right, preferred_element_type=jnp.float32)
    line = np.arange(TILE)
    own = jnp.where(jnp.asarray(line[:, None] < line[None, :]), own, 0.0)
    own = jnp.einsum("aiq,ceaij->ceaqj", hot_full, own, precision=high)
    own = jnp.einsum("ceaqj,ajs->ceasq", own, hot_full, precision=high)
    class_line = np.arange(CLASSES)
    back_u = class_line[:, None] // SPREAD - class_line[None, :] // SPREAD + SPREAD - 1
    back_v = class_line[:, None] % SPREAD - class_line[None, :] % SPREAD + SPREAD - 1
    pick = np.arange(seps * seps) == (back_u * seps + back_v).reshape(-1, 1)
    own = jnp.einsum(
        "ceam,mz->ceza",
        own.reshape(ch_dev, 2, tiles, CLASSES * CLASSES),
        jnp.asarray(pick.astype(np.float32)),
        precision=high,
    )
    diagonal = np.zeros((tiles, tiles * tiles), np.float32)
    diagonal[np.arange(tiles), np.arange(tiles) * (tiles + 1)] = 1.0
    own = jnp.einsum("ceza,ap->cezp", own, jnp.asarray(diagonal), precision=high)
    own = own.reshape(ch_dev, 2, seps, seps, tiles * tiles)
    same = jnp.asarray(diagonal.sum(axis=0) > 0)
    cross = jnp.where(same, own, cross)

    pair_first, pair_second = np.triu_indices(tiles)
    select = np.zeros((pair_first.size, tiles * tiles), np.float32)
    select[np.arange(pair_first.size), pair_second * tiles + pair_first] = 1.0
    missing = (1.0 - select.sum(axis=0)).astype(np.int32) * 4096
    cells = jnp.einsum(
        "cxk,kp->cxp", tile_cells.astype(jnp.float32), jnp.asarray(select), precision=highest
    )
    cells = jnp.round(cells).astype(jnp.int32) + jnp.asarray(missing)
    weights = jnp.stack(
        [separation_table(first_chan + i, divisor, kernel_table)[::-1] for i in range(ch_dev)]
    )
    rows = shifted_weights(weights * norm_factor, cells[:, 0])
    cols = shifted_weights(weights, cells[:, 1])
    spread_cols = sum(
        cross[:, :, :, v, None, :] * cols[:, None, None, v] for v in range(seps)
    )
    planes = jnp.einsum("cdup,cedwp->ucew", rows, spread_cols, precision=high)
    grid_count = lax.axis_size("grid")
    planes = planes.reshape(grid_count, UV // grid_count, ch_dev, 2 * UV).astype(jnp.bfloat16)
    parts = lax.all_to_all(planes, "grid", split_axis=0, concat_axis=0, tiled=True)
    return parts.astype(jnp.float32).sum(axis=0)


def solution(mesh):
    placed = (P("stn", None, "grid"), P(), P(), P("stn", None, None), P())
    return jax.shard_map(
        body, mesh=mesh, in_specs=placed, out_specs=P("grid", "stn", None), check_vma=False
    )
```

```python
import math

import jax
import jax.numpy as jnp
import numpy as np
from jax import lax
from jax.sharding import PartitionSpec as P

TILE = 32
PATCH = 16
SPREAD = 5
UV = 128


highest = lax.Precision.HIGHEST


def shifted(block, axis, distance):
    devices = range(lax.axis_size(axis))
    route = [(i - distance, i) for i in devices if i - distance in devices]
    return lax.ppermute(block, axis, route)


def dft_table(frame_len):
    chan_count = frame_len // 2
    sample_line = jnp.arange(frame_len, dtype=jnp.int32)[:, None]
    chan_line = jnp.arange(chan_count, dtype=jnp.int32)[None, :]
    angles = (sample_line * chan_line % frame_len).astype(jnp.float32) * (2.0 * math.pi / frame_len)
    norm_factor = 1.0 / math.sqrt(frame_len)
    twiddle = jnp.stack([jnp.cos(angles) * norm_factor, -jnp.sin(angles) * norm_factor], axis=2)
    return twiddle.reshape(frame_len, 2 * chan_count).astype(jnp.bfloat16)


CLASSES = SPREAD * SPREAD
high = lax.Precision.HIGH


def fused_filter(coeffs, twiddle, step):
    taps, frame_len = coeffs.shape
    flat = coeffs.reshape(-1)
    columns = [
        jnp.pad(flat, (frame_len * (f + 1), frame_len * (step - 1 - f))) for f in range(step)
    ]
    shifted_coeffs = jnp.stack(columns, axis=0)
    spread = np.kron(np.ones((1, frame_len), np.float32), np.eye(step, dtype=np.float32))
    wide = jnp.einsum("fm,fn->mn", shifted_coeffs, jnp.asarray(spread), precision=highest)
    tiled = jnp.tile(jnp.repeat(twiddle.astype(jnp.float32), step, axis=1), (step + taps, 1))
    return (wide * tiled).astype(jnp.bfloat16)

def separation_table(frequency, divisor, kernel_table):
    over_count = kernel_table.shape[0]
    separation = jnp.arange(2 * SPREAD - 1, dtype=jnp.int32)
    scaled = separation * frequency
    cell_index = scaled // divisor
    fine_index = scaled % divisor * over_count // divisor
    choose = (fine_index[:, None] == jnp.arange(over_count, dtype=jnp.int32)[None, :]).astype(
        jnp.float32
    )
    tap_values = jnp.dot(choose, kernel_table, precision=highest)
    place_rel = jnp.arange(PATCH, dtype=jnp.int32)[None, :] - cell_index[:, None]
    weights = jnp.zeros(place_rel.shape, jnp.float32)
    for tap_index in range(kernel_table.shape[1]):
        weights = weights + tap_values[:, tap_index : tap_index + 1] * (
            place_rel == tap_index
        ).astype(jnp.float32)
    return weights


def shifted_weights(weights, bases):
    place = jnp.arange(UV, dtype=jnp.int32)[None, :, None] - bases[:, None, :]
    taps = jnp.arange(PATCH, dtype=jnp.int32)[None, :, None, None]
    spots = place[:, None] == taps
    if weights.dtype == jnp.float32:
        return jnp.einsum("cdt,ctwp->cdwp", weights, spots.astype(jnp.float32), precision=highest)
    return jnp.einsum(
        "cdt,ctwp->cdwp", weights, spots.astype(jnp.bfloat16), preferred_element_type=jnp.float32
    ).astype(jnp.bfloat16)


def body(voltages, pfb_coeffs, station_offsets, tile_cells, kernel_table):
    stn_local, pol_count, samples = voltages.shape
    tap_count, frame_len = pfb_coeffs.shape
    spec_count = samples // frame_len
    step = 128 // math.gcd(128, frame_len)
    chunks = spec_count // step
    flat = jnp.transpose(voltages, (1, 0, 2))
    earlier = shifted(flat[:, :, samples - tap_count * frame_len :], "grid", 1)
    extended = jnp.concatenate([earlier, flat], axis=2)
    width = step * frame_len
    reach = (step + tap_count) * frame_len
    blocks = jnp.stack(
        [extended[:, :, c * width : c * width + reach] for c in range(chunks)], axis=1
    )
    matrix = fused_filter(pfb_coeffs, dft_table(frame_len), step)
    spectra = jnp.einsum(
        "pcsm,mn->npcs", blocks, matrix, preferred_element_type=jnp.float32
    ).astype(jnp.bfloat16)
    spectra = spectra.reshape(frame_len // 2, 2, step * pol_count * chunks, stn_local)
    turned = lax.all_to_all(spectra, "stn", split_axis=0, concat_axis=3, tiled=True)
    turned = jnp.transpose(turned, (0, 1, 3, 2))
    ch_dev, _, stations, depth = turned.shape
    tiles = stations // TILE
    divisor = frame_len - 1
    first_chan = lax.axis_index("stn") * ch_dev + frame_len // 2
    norm_factor = 1.0 / (pol_count * spec_count * lax.axis_size("grid"))

    classes = (station_offsets[0] * SPREAD + station_offsets[1]).reshape(tiles, TILE)
    hot = classes[:, :, None] == jnp.arange(CLASSES, dtype=jnp.int32)
    hot_low = hot.astype(jnp.bfloat16)
    hot_full = hot.astype(jnp.float32)
    tiled = turned.reshape(ch_dev, 2, tiles, TILE, depth)
    summed = jnp.einsum(
        "aiq,ceaik->ceaqk", hot_low, tiled, preferred_element_type=jnp.float32
    ).astype(jnp.bfloat16)

    def stacked(z):
        real_part, imag_part = z[:, 0], z[:, 1]
        partner = jnp.concatenate([real_part, imag_part], axis=-1)
        turned_partner = jnp.concatenate([imag_part, -real_part], axis=-1)
        return jnp.stack([partner, turned_partner], axis=1), partner

    left, right = stacked(summed)
    shape = (SPREAD, SPREAD, 2 * depth)
    terms = []
    for i in range(ch_dev):
        taps = jnp.transpose(left[i].reshape((2 * tiles,) + shape), (1, 2, 3, 0))
        terms.append(
            lax.conv_general_dilated(
                right[i].reshape((tiles,) + shape),
                taps,
                (1, 1),
                [(SPREAD - 1, SPREAD - 1)] * 2,
                dimension_numbers=("NHWC", "HWIO", "HWNC"),
                preferred_element_type=jnp.float32,
            )
        )
    seps = 2 * SPREAD - 1
    cross = jnp.stack(terms).reshape(ch_dev, seps, seps, tiles, 2, tiles)
    cross = jnp.transpose(cross, (0, 4, 1, 2, 3, 5)).reshape(ch_dev, 2, seps, seps, tiles * tiles)
    own_left, own_right = stacked(tiled)
    own = jnp.einsum("ceaik,cajk->ceaij", own_left, own_right, preferred_element_type=jnp.float32)
    line = np.arange(TILE)
    own = jnp.where(jnp.asarray(line[:, None] < line[None, :]), own, 0.0)
    own = jnp.einsum("aiq,ceaij->ceaqj", hot_full, own, precision=high)
    own = jnp.einsum("ceaqj,ajs->ceasq", own, hot_full, precision=high)
    class_line = np.arange(CLASSES)
    back_u = class_line[:, None] // SPREAD - class_line[None, :] // SPREAD + SPREAD - 1
    back_v = class_line[:, None] % SPREAD - class_line[None, :] % SPREAD + SPREAD - 1
    pick = np.arange(seps * seps) == (back_u * seps + back_v).reshape(-1, 1)
    own = jnp.einsum(
        "ceam,mz->ceza",
        own.reshape(ch_dev, 2, tiles, CLASSES * CLASSES),
        jnp.asarray(pick.astype(np.float32)),
        precision=high,
    )
    diagonal = np.zeros((tiles, tiles * tiles), np.float32)
    diagonal[np.arange(tiles), np.arange(tiles) * (tiles + 1)] = 1.0
    own = jnp.einsum("ceza,ap->cezp", own, jnp.asarray(diagonal), precision=high)
    own = own.reshape(ch_dev, 2, seps, seps, tiles * tiles)
    same = jnp.asarray(diagonal.sum(axis=0) > 0)
    cross = jnp.where(same, own, cross)

    pair_first, pair_second = np.triu_indices(tiles)
    select = np.zeros((pair_first.size, tiles * tiles), np.float32)
    select[np.arange(pair_first.size), pair_second * tiles + pair_first] = 1.0
    missing = (1.0 - select.sum(axis=0)).astype(np.int32) * 4096
    cells = jnp.einsum(
        "cxk,kp->cxp", tile_cells.astype(jnp.float32), jnp.asarray(select), precision=highest
    )
    cells = jnp.round(cells).astype(jnp.int32) + jnp.asarray(missing)
    weights = jnp.stack(
        [separation_table(first_chan + i, divisor, kernel_table)[::-1] for i in range(ch_dev)]
    )
    scaled = weights * norm_factor
    coarse = lax.reduce_precision(scaled, 8, 7)
    rest = (scaled - coarse).astype(jnp.bfloat16)
    rows = [shifted_weights(part, cells[:, 0]) for part in (coarse.astype(jnp.bfloat16), rest)]
    cols = shifted_weights(weights, cells[:, 1])
    spread_cols = sum(
        cross[:, :, :, v, None, :] * cols[:, None, None, v] for v in range(seps)
    )
    spread_cols = spread_cols.astype(jnp.bfloat16)
    planes = sum(
        jnp.einsum(
            "cdup,cedwp->ucew", part, spread_cols, preferred_element_type=jnp.float32
        )
        for part in rows
    )
    grid_count = lax.axis_size("grid")
    planes = planes.reshape(grid_count, UV // grid_count, ch_dev, 2 * UV).astype(jnp.bfloat16)
    parts = lax.all_to_all(planes, "grid", split_axis=0, concat_axis=0, tiled=True)
    return parts.astype(jnp.float32).sum(axis=0)


def solution(mesh):
    placed = (P("stn", None, "grid"), P(), P(), P("stn", None, None), P())
    return jax.shard_map(
        body, mesh=mesh, in_specs=placed, out_specs=P("grid", "stn", None), check_vma=False
    )
```

```python
import math

import jax
import jax.numpy as jnp
import numpy as np
from jax import lax
from jax.sharding import PartitionSpec as P

TILE = 32
PATCH = 16
SPREAD = 5
UV = 128


highest = lax.Precision.HIGHEST


def shifted(block, axis, distance):
    devices = range(lax.axis_size(axis))
    route = [(i - distance, i) for i in devices if i - distance in devices]
    return lax.ppermute(block, axis, route)


def dft_table(frame_len):
    chan_count = frame_len // 2
    sample_line = jnp.arange(frame_len, dtype=jnp.int32)[:, None]
    chan_line = jnp.arange(chan_count, dtype=jnp.int32)[None, :]
    angles = (sample_line * chan_line % frame_len).astype(jnp.float32) * (2.0 * math.pi / frame_len)
    norm_factor = 1.0 / math.sqrt(frame_len)
    twiddle = jnp.stack([jnp.cos(angles) * norm_factor, -jnp.sin(angles) * norm_factor], axis=2)
    return twiddle.reshape(frame_len, 2 * chan_count).astype(jnp.bfloat16)


CLASSES = SPREAD * SPREAD
high = lax.Precision.HIGH


def fused_filter(coeffs, twiddle, step):
    taps, frame_len = coeffs.shape
    flat = coeffs.reshape(-1)
    columns = [
        jnp.pad(flat, (frame_len * (f + 1), frame_len * (step - 1 - f))) for f in range(step)
    ]
    shifted_coeffs = jnp.stack(columns, axis=0)
    spread = np.kron(np.ones((1, frame_len), np.float32), np.eye(step, dtype=np.float32))
    wide = jnp.einsum("fm,fn->mn", shifted_coeffs, jnp.asarray(spread), precision=highest)
    tiled = jnp.tile(jnp.repeat(twiddle.astype(jnp.float32), step, axis=1), (step + taps, 1))
    return (wide * tiled).astype(jnp.bfloat16)

def separation_table(frequency, divisor, kernel_table):
    over_count = kernel_table.shape[0]
    separation = jnp.arange(2 * SPREAD - 1, dtype=jnp.int32)
    scaled = separation * frequency
    cell_index = scaled // divisor
    fine_index = scaled % divisor * over_count // divisor
    choose = (fine_index[:, None] == jnp.arange(over_count, dtype=jnp.int32)[None, :]).astype(
        jnp.float32
    )
    tap_values = jnp.dot(choose, kernel_table, precision=highest)
    place_rel = jnp.arange(PATCH, dtype=jnp.int32)[None, :] - cell_index[:, None]
    weights = jnp.zeros(place_rel.shape, jnp.float32)
    for tap_index in range(kernel_table.shape[1]):
        weights = weights + tap_values[:, tap_index : tap_index + 1] * (
            place_rel == tap_index
        ).astype(jnp.float32)
    return weights


def shifted_weights(weights, bases):
    place = jnp.arange(UV, dtype=jnp.int32)[None, :, None] - bases[:, None, :]
    taps = jnp.arange(PATCH, dtype=jnp.int32)[None, :, None, None]
    spots = place[:, None] == taps
    if weights.dtype == jnp.float32:
        return jnp.einsum("cdt,ctwp->cdwp", weights, spots.astype(jnp.float32), precision=highest)
    return jnp.einsum(
        "cdt,ctwp->cdwp", weights, spots.astype(jnp.bfloat16), preferred_element_type=jnp.float32
    ).astype(jnp.bfloat16)


def body(voltages, pfb_coeffs, station_offsets, tile_cells, kernel_table):
    stn_local, pol_count, samples = voltages.shape
    tap_count, frame_len = pfb_coeffs.shape
    spec_count = samples // frame_len
    step = 128 // math.gcd(128, frame_len)
    chunks = spec_count // step
    flat = jnp.transpose(voltages, (1, 0, 2))
    earlier = shifted(flat[:, :, samples - tap_count * frame_len :], "grid", 1)
    extended = jnp.concatenate([earlier, flat], axis=2)
    width = step * frame_len
    reach = (step + tap_count) * frame_len
    blocks = jnp.stack(
        [extended[:, :, c * width : c * width + reach] for c in range(chunks)], axis=1
    )
    matrix = fused_filter(pfb_coeffs, dft_table(frame_len), step)
    spectra = jnp.einsum(
        "pcsm,mn->npcs", blocks, matrix, preferred_element_type=jnp.float32
    ).astype(jnp.bfloat16)
    spectra = spectra.reshape(frame_len // 2, 2, step * pol_count * chunks, stn_local)
    spectra, tile_cells = lax.optimization_barrier((spectra, tile_cells))
    turned = lax.all_to_all(spectra, "stn", split_axis=0, concat_axis=3, tiled=True)
    turned = jnp.transpose(turned, (0, 1, 3, 2))
    ch_dev, _, stations, depth = turned.shape
    tiles = stations // TILE
    divisor = frame_len - 1
    first_chan = lax.axis_index("stn") * ch_dev + frame_len // 2
    norm_factor = 1.0 / (pol_count * spec_count * lax.axis_size("grid"))

    classes = (station_offsets[0] * SPREAD + station_offsets[1]).reshape(tiles, TILE)
    hot = classes[:, :, None] == jnp.arange(CLASSES, dtype=jnp.int32)
    hot_low = hot.astype(jnp.bfloat16)
    hot_full = hot.astype(jnp.float32)
    tiled = turned.reshape(ch_dev, 2, tiles, TILE, depth)
    summed = jnp.einsum(
        "aiq,ceaik->ceaqk", hot_low, tiled, preferred_element_type=jnp.float32
    ).astype(jnp.bfloat16)

    def stacked(z):
        real_part, imag_part = z[:, 0], z[:, 1]
        partner = jnp.concatenate([real_part, imag_part], axis=-1)
        turned_partner = jnp.concatenate([imag_part, -real_part], axis=-1)
        return jnp.stack([partner, turned_partner], axis=1), partner

    left, right = stacked(summed)
    shape = (SPREAD, SPREAD, 2 * depth)
    terms = []
    for i in range(ch_dev):
        taps = jnp.transpose(left[i].reshape((2 * tiles,) + shape), (1, 2, 3, 0))
        terms.append(
            lax.conv_general_dilated(
                right[i].reshape((tiles,) + shape),
                taps,
                (1, 1),
                [(SPREAD - 1, SPREAD - 1)] * 2,
                dimension_numbers=("NHWC", "HWIO", "HWNC"),
                preferred_element_type=jnp.float32,
            )
        )
    seps = 2 * SPREAD - 1
    cross = jnp.stack(terms).reshape(ch_dev, seps, seps, tiles, 2, tiles)
    cross = jnp.transpose(cross, (0, 4, 1, 2, 3, 5)).reshape(ch_dev, 2, seps, seps, tiles * tiles)
    own_left, own_right = stacked(tiled)
    own = jnp.einsum("ceaik,cajk->ceaij", own_left, own_right, preferred_element_type=jnp.float32)
    line = np.arange(TILE)
    own = jnp.where(jnp.asarray(line[:, None] < line[None, :]), own, 0.0)
    own = jnp.einsum("aiq,ceaij->ceaqj", hot_full, own, precision=high)
    own = jnp.einsum("ceaqj,ajs->ceasq", own, hot_full, precision=high)
    class_line = np.arange(CLASSES)
    back_u = class_line[:, None] // SPREAD - class_line[None, :] // SPREAD + SPREAD - 1
    back_v = class_line[:, None] % SPREAD - class_line[None, :] % SPREAD + SPREAD - 1
    pick = np.arange(seps * seps) == (back_u * seps + back_v).reshape(-1, 1)
    own = jnp.einsum(
        "ceam,mz->ceza",
        own.reshape(ch_dev, 2, tiles, CLASSES * CLASSES),
        jnp.asarray(pick.astype(np.float32)),
        precision=high,
    )
    diagonal = np.zeros((tiles, tiles * tiles), np.float32)
    diagonal[np.arange(tiles), np.arange(tiles) * (tiles + 1)] = 1.0
    own = jnp.einsum("ceza,ap->cezp", own, jnp.asarray(diagonal), precision=high)
    own = own.reshape(ch_dev, 2, seps, seps, tiles * tiles)
    same = jnp.asarray(diagonal.sum(axis=0) > 0)
    cross = jnp.where(same, own, cross)

    pair_first, pair_second = np.triu_indices(tiles)
    select = np.zeros((pair_first.size, tiles * tiles), np.float32)
    select[np.arange(pair_first.size), pair_second * tiles + pair_first] = 1.0
    missing = (1.0 - select.sum(axis=0)).astype(np.int32) * 4096
    cells = jnp.einsum(
        "cxk,kp->cxp", tile_cells.astype(jnp.float32), jnp.asarray(select), precision=highest
    )
    cells = jnp.round(cells).astype(jnp.int32) + jnp.asarray(missing)
    weights = jnp.stack(
        [separation_table(first_chan + i, divisor, kernel_table)[::-1] for i in range(ch_dev)]
    )
    scaled = weights * norm_factor
    coarse = lax.reduce_precision(scaled, 8, 7)
    rest = (scaled - coarse).astype(jnp.bfloat16)
    rows = [shifted_weights(part, cells[:, 0]) for part in (coarse.astype(jnp.bfloat16), rest)]
    place = jnp.arange(UV, dtype=jnp.int32)[None, :, None] - cells[:, 1][:, None, :]
    cols = []
    for v in range(seps):
        placed = jnp.zeros(place.shape, jnp.float32)
        for t in range(PATCH):
            placed = jnp.where(place == t, weights[:, v, t][:, None, None], placed)
        cols.append(placed)
    cols = lax.optimization_barrier(tuple(cols))
    spread_cols = sum(
        cross[:, :, :, v, None, :] * cols[v][:, None, None] for v in range(seps)
    )
    spread_cols = spread_cols.astype(jnp.bfloat16)
    planes = sum(
        jnp.einsum(
            "cdup,cedwp->ucew", part, spread_cols, preferred_element_type=jnp.float32
        )
        for part in rows
    )
    grid_count = lax.axis_size("grid")
    planes = planes.reshape(grid_count, UV // grid_count, ch_dev, 2 * UV).astype(jnp.bfloat16)
    parts = lax.all_to_all(planes, "grid", split_axis=0, concat_axis=0, tiled=True)
    return parts.astype(jnp.float32).sum(axis=0)


def solution(mesh):
    placed = (P("stn", None, "grid"), P(), P(), P("stn", None, None), P())
    return jax.shard_map(
        body, mesh=mesh, in_specs=placed, out_specs=P("grid", "stn", None), check_vma=False
    )
```
